128 devices in a mesh: dp: 8 (over y_lo, z), ctx: 16 (over y_hi, x, core).
Axes of the slice: x: 4, y: 4 (y_hi: 2, y_lo: 2; y = y_hi * 2 + y_lo), z: 4, core: 2. Of those that a mesh axis runs over, the one named last changes fastest.
Arguments:
- tokens: bfloat16 [16384, 768], P(('dp', 'ctx')), may hold values from -6 to 6
- cotangent: bfloat16 [16384, 768], P(('dp', 'ctx')), may hold values from -6 to 6
- w_qkv: bfloat16 [2, 768, 2304], P(None, 'dp'), may hold values from -0.21875 to 0.21875
- w_out: bfloat16 [2, 768, 768], P(None, 'dp'), may hold values from -0.875 to 0.875
- w_up: bfloat16 [2, 768, 3072], P(None, 'dp'), may hold values from -0.21875 to 0.21875
- w_down: bfloat16 [2, 3072, 768], P(None, 'dp'), may hold values from -0.109375 to 0.109375
- gains: bfloat16 [2, 2, 768], P(None, None, 'dp'), may hold values from 0.099609375 to 1.8984375
- shifts: bfloat16 [2, 6, 768], P(None, None, 'dp'), may hold values from -3 to 3
- up_bias: bfloat16 [2, 3072], P(None, 'dp'), may hold values from -3 to 3
Outputs:
- output: bfloat16 [16384, 768], P(('dp', 'ctx'))
- grad_tokens: float32 [16384, 768], P(('dp', 'ctx'))
- grad_qkv: float32 [2, 768, 2304], P(None, 'dp')
- grad_out: float32 [2, 768, 768], P(None, 'dp')
- grad_up: float32 [2, 768, 3072], P(None, 'dp')
- grad_down: float32 [2, 3072, 768], P(None, 'dp')
- grad_gains: float32 [2, 2, 768], P(None, None, 'dp')
- grad_shifts: float32 [2, 6, 768], P(None, None, 'dp')
- grad_upbias: float32 [2, 3072], P(None, 'dp')
The draws below stay inside these ranges and needn't reach their ends.
All inputs are finite; a program needn't handle non-finite values.
Results may differ from the reference program's by a relative error of at most 0.023.
Values may be sent and summed in bfloat16 or wider, within the bound.
No kernel may reach another device: no remote copies, remote signals or barrier semaphores. Data moves between devices by JAX's collectives and lax.ppermute only.
A program may use at most 192 MiB of HBM per device.

```python
import jax
import jax.numpy as jnp
from jax import lax

D = 768
HEADS = 12
HEAD = 64
FF = 3072
LAYERS = 2
BLK = 128
TOKENS = 16384
N_DP = 8
N_CTX = 16


def levels(rng, extent, shards, least, high):
    level = 1.0
    for axis_at, shards_of in shards:
        heights = jax.random.uniform(jax.random.fold_in(jax.random.fold_in(rng, 6), axis_at), (shards_of,), jnp.float32, least / len(shards), high / len(shards))
        level = level * jnp.repeat(jnp.exp(heights), extent[axis_at] // shards_of).reshape((-1,) + (1,) * (len(extent) - 1 - axis_at))
    return level


def scatter_about(key, shape, scale, most, shards=(), held_as=jnp.bfloat16):
    entries = scale * jax.random.normal(key, shape, jnp.float32)
    if shards:
        entries = entries * levels(key, shape, shards, -0.22, 0.18)
    return jnp.clip(entries, -most, most).astype(held_as)


def setup_inputs(seed: int = 0) -> dict:
    streams_of = jax.random.split(jax.random.key(seed), 10)
    tokens = scatter_about(streams_of[0], (TOKENS, D), 1.0, 6.0, ((0, 128),))
    cotangent = scatter_about(streams_of[1], (TOKENS, D), 1.0, 6.0, ((0, 128),))
    w_qkv = scatter_about(streams_of[2], (LAYERS, D, 3 * D), D ** -0.5, 0.21875, ((1, 8),))
    w_out = scatter_about(streams_of[3], (LAYERS, D, D), (D // 16) ** -0.5, 0.875, ((1, 8),))
    w_up = scatter_about(streams_of[4], (LAYERS, D, FF), D ** -0.5, 0.21875, ((1, 8),))
    w_down = scatter_about(streams_of[5], (LAYERS, FF, D), FF ** -0.5, 0.109375, ((1, 8),))
    gains = jnp.clip(1.0 + 0.18 * jax.random.normal(streams_of[6], (LAYERS, 2, D), jnp.float32), 0.099609375, 1.8984375).astype(jnp.bfloat16)
    shifts = scatter_about(streams_of[7], (LAYERS, 6, D), 0.5, 3.0, ((2, 8),))
    up_bias = scatter_about(streams_of[8], (LAYERS, FF), 0.5, 3.0, ((1, 8),))
    return dict(tokens=tokens, cotangent=cotangent, w_qkv=w_qkv, w_out=w_out, w_up=w_up, w_down=w_down, gains=gains, shifts=shifts, up_bias=up_bias)


EPSILON = 1e-05
NEGATIVE = -1e+30

@jax.custom_vjp
def low(v):
    return lax.optimization_barrier(v.astype(jnp.bfloat16)).astype(jnp.float32)

@jax.custom_vjp
def low_back(v):
    return v

def low_keep(v):
    return (low(v), None)

def low_pass(kept, grad):
    return (grad,)

def back_keep(v):
    return (v, None)

def back_low(kept, grad):
    return (low(grad),)
low.defvjp(low_keep, low_pass)
low_back.defvjp(back_keep, back_low)

def product(left, right):
    return jnp.dot(left, right, precision=lax.Precision.HIGHEST, preferred_element_type=jnp.float32)

def normalize(values, gain, shift):
    average = lax.optimization_barrier(jnp.mean(values, axis=-1, keepdims=True))
    centered = values - average
    spread = lax.optimization_barrier(jnp.mean(centered * centered, axis=-1, keepdims=True))
    return centered * lax.rsqrt(spread + EPSILON) * gain + shift

def attention(queries, keys, values):
    seq_len = queries.shape[0]
    block = min(512, seq_len)
    count = seq_len // block
    query_heads = queries.reshape(seq_len, HEADS, HEAD).transpose(1, 0, 2)
    key_heads = keys.reshape(seq_len, HEADS, HEAD).transpose(1, 0, 2)
    value_heads = values.reshape(seq_len, HEADS, HEAD).transpose(1, 0, 2)
    blocks = query_heads.reshape(HEADS, count, block, HEAD).transpose(1, 0, 2, 3)
    starts = (jnp.arange(count) * block).astype(jnp.int32)

    def one_block(query_block, start):
        scores = jnp.einsum('hqd,hkd->hqk', query_block, key_heads, precision=lax.Precision.HIGHEST)
        scores = low_back(scores)
        positions = (start + jnp.arange(block)).astype(jnp.int32)
        allowed = jnp.arange(seq_len).astype(jnp.int32)[None, :] <= positions[:, None]
        masked = jnp.where(allowed[None], scores, NEGATIVE)
        peak = lax.optimization_barrier(jnp.max(masked, axis=2, keepdims=True))
        weights = jnp.exp(masked - peak)
        probs = low(weights / lax.optimization_barrier(jnp.sum(weights, axis=2, keepdims=True)))
        return jnp.einsum('hqk,hkd->hqd', probs, value_heads, precision=lax.Precision.HIGHEST)
    checked = jax.checkpoint(one_block)

    def apply_block(packed):
        return checked(packed[0], packed[1])
    result = lax.map(apply_block, (blocks, starts))
    result = result.transpose(1, 0, 2, 3).reshape(HEADS, seq_len, HEAD)
    return result.transpose(1, 0, 2).reshape(seq_len, D)

def layer_forward(state, w_qkv, w_out, w_up, w_down, gains, shifts, up_bias):
    normed = low(normalize(state, gains[0], shifts[0]))
    bias_full = jnp.concatenate([shifts[2], jnp.zeros_like(shifts[2]), shifts[3]])
    mixed = low_back(product(normed, w_qkv) + bias_full)
    queries = low(mixed[:, :D] * HEAD ** (-0.5))
    keys = low(mixed[:, D:2 * D])
    values = low(mixed[:, 2 * D:])
    context = attention(queries, keys, values)
    attended = low(low_back(context))
    branch = low_back(product(attended, w_out) + shifts[4])
    middle = state + branch
    normed_two = low(normalize(middle, gains[1], shifts[1]))
    upper = low_back(product(normed_two, w_up) + up_bias)
    active = low(jax.nn.gelu(upper))
    branch_two = low_back(product(active, w_down) + shifts[5])
    return middle + branch_two

def forward_layers(state, w_qkv, w_out, w_up, w_down, gains, shifts, up_bias):
    for layer in range(LAYERS):
        state = layer_forward(state, w_qkv[layer], w_out[layer], w_up[layer], w_down[layer], gains[layer], shifts[layer], up_bias[layer])
    return state

def reference(tokens, cotangent, w_qkv, w_out, w_up, w_down, gains, shifts, up_bias):
    params = (w_qkv.astype(jnp.float32), w_out.astype(jnp.float32), w_up.astype(jnp.float32), w_down.astype(jnp.float32), gains.astype(jnp.float32), shifts.astype(jnp.float32), up_bias.astype(jnp.float32))
    seq_len = BLK * N_CTX
    inputs = tokens.astype(jnp.float32).reshape(N_DP, seq_len, D)
    cotangents = cotangent.astype(jnp.float32).reshape(N_DP, seq_len, D)

    def one_sequence(totals, sample):
        sequence, seq_cot = sample
        result, backward = jax.vjp(forward_layers, sequence, *params)
        gradients = backward(seq_cot)
        totals = tuple((summed + added for summed, added in zip(totals, gradients[1:])))
        return (totals, (result.astype(jnp.bfloat16), gradients[0]))
    zero_grads = tuple((jnp.zeros_like(weight) for weight in params))
    totals, (outputs, grad_inputs) = lax.scan(one_sequence, zero_grads, (inputs, cotangents))
    return (outputs.reshape(N_DP * seq_len, D), grad_inputs.reshape(N_DP * seq_len, D), totals[0], totals[1], totals[2], totals[3], totals[4], totals[5], totals[6])
```

```python
import jax
import jax.numpy as jnp
from jax import lax
from jax.experimental import pallas as pl
from jax.experimental.pallas import tpu as pltpu
from jax.sharding import PartitionSpec as P

HEADS = 12
HEAD = 64
LAYERS = 2
D = 768
FF = 3072
DP = 8
BLK = 128
CHIPS = 8
CORES = 2
PAIR = CORES * BLK
OWN_HEADS = HEADS // CORES
SEQ = CHIPS * PAIR
FF_PART = FF // DP // CORES
FF_HALF = FF // CORES
QKV_HALF = 3 * D // CORES
PIECE = 640
EPSILON = 1e-05
NEGATIVE = -1e30
SAME_CORE = [[CORES * u + k for u in range(CHIPS)] for k in range(CORES)]
OTHER_CORE = [(i, i ^ 1) for i in range(CHIPS * CORES)]
BF = jnp.bfloat16
F32 = jnp.float32


def dot(left, right, ldim, rdim):
    return lax.dot_general(
        left, right, (((ldim,), (rdim,)), ((), ())), preferred_element_type=F32
    )


def swap(value):
    return lax.ppermute(value, "ctx", OTHER_CORE)


def diagonal_mask(size):
    key = lax.broadcasted_iota(jnp.int32, (size, size), 0)
    query = lax.broadcasted_iota(jnp.int32, (size, size), 1)
    return key <= query


def attend_kernel(qkv_ref, out_ref, ctx_ref, lse_ref):
    step = PAIR
    keys = [qkv_ref[j, HEAD : 2 * HEAD, :] for j in range(CHIPS)]
    allowed = diagonal_mask(step)
    for i in range(CHIPS):
        query = qkv_ref[i, 0:HEAD, :]
        scores = [dot(keys[j], query, 0, 0) for j in range(i + 1)]
        scores[i] = jnp.where(allowed, scores[i], NEGATIVE)
        peak = scores[0].max(axis=0, keepdims=True)
        for j in range(1, i + 1):
            peak = jnp.maximum(peak, scores[j].max(axis=0, keepdims=True))
        total = jnp.zeros((1, step), F32)
        accum = jnp.zeros((HEAD, step), F32)
        for j in range(i + 1):
            weights = jnp.exp(scores[j] - peak)
            total = total + weights.sum(axis=0, keepdims=True)
            accum = accum + dot(qkv_ref[j, 2 * HEAD : 3 * HEAD, :], weights.astype(BF), 1, 0)
        context = accum / total
        out_ref[2 * i] = context[:, :BLK].astype(BF)
        out_ref[2 * i + 1] = context[:, BLK:].astype(BF)
        ctx_ref[i] = context
        lse_ref[i] = peak + jnp.log(total)


def attend(qkv):
    return pl.pallas_call(
        attend_kernel,
        out_shape=(
            jax.ShapeDtypeStruct((CORES * CHIPS, HEAD, BLK), BF),
            jax.ShapeDtypeStruct((CHIPS, HEAD, PAIR), F32),
            jax.ShapeDtypeStruct((CHIPS, 1, PAIR), F32),
        ),
        compiler_params=pltpu.CompilerParams(vmem_limit_bytes=40 * 1024 * 1024),
        name="attend",
    )(qkv)


def attend_back_kernel(qkv_ref, grad_ref, ctx_ref, lse_ref, out_ref, dq_ref):
    allowed = diagonal_mask(PAIR)
    grads, deltas = [], []
    for i in range(CHIPS):
        grad = jnp.concatenate([grad_ref[2 * i], grad_ref[2 * i + 1]], axis=1)
        grads.append(grad)
        deltas.append((grad.astype(F32) * ctx_ref[i]).sum(axis=0, keepdims=True))
    for j in range(CHIPS):
        key = qkv_ref[j, HEAD : 2 * HEAD, :]
        value = qkv_ref[j, 2 * HEAD : 3 * HEAD, :]
        grad_key = jnp.zeros((HEAD, PAIR), F32)
        grad_value = jnp.zeros((HEAD, PAIR), F32)
        for i in range(j, CHIPS):
            query = qkv_ref[i, 0:HEAD, :]
            probs = jnp.exp(dot(key, query, 0, 0) - lse_ref[i])
            if i == j:
                probs = jnp.where(allowed, probs, 0.0)
            grad_probs = dot(value, grads[i], 0, 0)
            grad_scores = (probs * (grad_probs - deltas[i])).astype(BF)
            grad_value = grad_value + dot(grads[i], probs.astype(BF), 1, 1)
            grad_key = grad_key + dot(query, grad_scores, 1, 1)
            grad_query = dot(key, grad_scores, 1, 0)
            if j == 0:
                dq_ref[i] = grad_query
            else:
                dq_ref[i] = dq_ref[i] + grad_query
        out_ref[j, 0:HEAD, :] = (dq_ref[j] * HEAD**-0.5).astype(BF)
        out_ref[j, HEAD : 2 * HEAD, :] = grad_key.astype(BF)
        out_ref[j, 2 * HEAD : 3 * HEAD, :] = grad_value.astype(BF)


def attend_back(qkv, grad, context, logsum):
    return pl.pallas_call(
        attend_back_kernel,
        out_shape=jax.ShapeDtypeStruct((CHIPS, 3 * HEAD, PAIR), BF),
        scratch_shapes=[pltpu.VMEM((CHIPS, HEAD, PAIR), F32)],
        compiler_params=pltpu.CompilerParams(vmem_limit_bytes=40 * 1024 * 1024),
        name="attend_back",
    )(qkv, grad, context, logsum)


def norm_parts(values):
    average = jnp.mean(values, axis=-1, keepdims=True)
    centered = values - average
    spread = jnp.mean(centered * centered, axis=-1, keepdims=True)
    scale = lax.rsqrt(spread + EPSILON)
    return centered * scale, scale


def norm_back(grad, hat, scale, gain):
    scaled = grad * gain
    first = jnp.mean(scaled, axis=-1, keepdims=True)
    second = jnp.mean(scaled * hat, axis=-1, keepdims=True)
    part = scale * (scaled - first - hat * second)
    return part, jnp.sum(grad * hat, axis=0), jnp.sum(grad, axis=0)


def ordered(mine, other, core):
    three = jnp.concatenate([mine, other, mine], axis=0)
    return lax.dynamic_slice_in_dim(three, core * BLK, PAIR, 0)


def across_chips(value):
    return lax.all_to_all(value, "ctx", 0, 0, axis_index_groups=SAME_CORE, tiled=True)


def layer_forward(state, weights, core):
    w_qkv, w_out, w_up, w_down, gains, shifts, qkv_bias, up_bias = weights
    hat_one, scale_one = norm_parts(state)
    mine = (hat_one * gains[0] + shifts[0]).astype(BF)
    normed = ordered(mine, swap(mine), core)
    mixed = (dot(w_qkv, normed, 0, 1) + qkv_bias[:, None]).reshape(OWN_HEADS, 3, HEAD, PAIR)
    factor = jnp.array([HEAD**-0.5, 1.0, 1.0], F32).reshape(1, 3, 1, 1)
    qkv = (mixed * factor).astype(BF).reshape(OWN_HEADS, 3 * HEAD, PAIR)
    qkv = jnp.concatenate([qkv, jnp.zeros((CHIPS - OWN_HEADS, 3 * HEAD, PAIR), BF)], axis=0)
    qkv = across_chips(qkv)
    out, context, logsum = attend(qkv)
    out = lax.all_to_all(out, "ctx", 0, 0, tiled=True)
    attended = out[:HEADS].reshape(D, BLK)
    middle = state + (dot(attended, w_out, 0, 0) + shifts[4])
    hat_two, scale_two = norm_parts(middle)
    mine_two = (hat_two * gains[1] + shifts[1]).astype(BF)
    normed_two = jnp.concatenate([mine_two, swap(mine_two)], axis=0)
    upper = dot(normed_two, w_up, 1, 0) + up_bias
    active = jax.nn.gelu(upper).astype(BF)
    partial = dot(active, w_down, 1, 0)
    result = middle + (partial[:BLK] + swap(partial[BLK:].astype(BF)).astype(F32) + shifts[5])
    kept = (
        hat_one, scale_one, normed, qkv, context, logsum,
        attended, hat_two, scale_two, normed_two, upper, active,
    )
    return result, kept


def half_to_full(vector, parts, core):
    piece = vector.reshape(parts, 1, -1)
    slot = lax.broadcasted_iota(jnp.int32, (parts, CORES, piece.shape[2]), 1)
    return jnp.where(slot == core, piece, 0.0).reshape(-1)


def layer_backward(kept, weights, grad_result, core):
    (
        hat_one, scale_one, normed, qkv, context, logsum,
        attended, hat_two, scale_two, normed_two, upper, active,
    ) = kept
    w_qkv, w_out, w_up, w_down, gains, shifts, qkv_bias, up_bias = weights
    mine = grad_result.astype(BF)
    down_bias = jnp.sum(mine.astype(F32), axis=0)
    both = jnp.concatenate([mine, swap(mine)], axis=0)
    grad_active = dot(both, w_down, 1, 1)
    gelu_back = jax.vjp(jax.nn.gelu, upper)[1]
    grad_upper = gelu_back(grad_active)[0].astype(BF)
    partial = dot(grad_upper, w_up, 1, 1)
    grad_normed_two = partial[:BLK] + swap(partial[BLK:].astype(BF)).astype(F32)
    grad_down = dot(active, both, 0, 0).astype(BF)
    grad_up = dot(normed_two, grad_upper, 0, 0).astype(BF)
    grad_upbias = jnp.sum(grad_upper.astype(F32), axis=0)
    shares_up = lax.psum_scatter(grad_up, "dp", scatter_dimension=0, tiled=True)
    shares_down = lax.psum_scatter(grad_down, "dp", scatter_dimension=0, tiled=True)
    part, gain_two, shift_two = norm_back(grad_normed_two, hat_two, scale_two, gains[1])
    grad_middle = grad_result + part
    branch = grad_middle.astype(BF)
    out_bias = jnp.sum(branch.astype(F32), axis=0)
    grad_out_t = dot(w_out, branch, 1, 1).astype(BF).reshape(HEADS, HEAD, BLK)
    grad_out_t = jnp.concatenate(
        [grad_out_t, jnp.zeros((CHIPS * CORES - HEADS, HEAD, BLK), BF)], axis=0
    )
    grad_context = lax.all_to_all(grad_out_t, "ctx", 0, 0, tiled=True)
    grad_out = dot(attended, branch, 1, 0)
    grad_mixed = across_chips(attend_back(qkv, grad_context, context, logsum))
    grad_mixed = grad_mixed[:OWN_HEADS].reshape(QKV_HALF, PAIR)
    partial = dot(grad_mixed, w_qkv, 0, 1)
    mine = lax.dynamic_slice_in_dim(partial, core * BLK, BLK, 0)
    other = lax.dynamic_slice_in_dim(partial, (1 - core) * BLK, BLK, 0)
    grad_normed = mine + swap(other.astype(BF)).astype(F32)
    grad_qkv = dot(normed, grad_mixed, 0, 1).astype(BF)
    sums = jnp.sum(grad_mixed.astype(F32), axis=1).reshape(OWN_HEADS, 3, HEAD)
    part, gain_one, shift_one = norm_back(grad_normed, hat_one, scale_one, gains[0])
    grad_state = grad_middle + part
    columns = D // CORES
    keep = lax.dynamic_slice_in_dim(grad_out, core * columns, columns, 1)
    give = lax.dynamic_slice_in_dim(grad_out, (1 - core) * columns, columns, 1)
    grad_out = (keep + swap(give.astype(BF)).astype(F32)).astype(BF)
    upbias = half_to_full(grad_upbias, DP, core).reshape(DP, 4, D // DP)
    upbias = upbias.transpose(1, 0, 2).reshape(4, D)
    small = jnp.stack(
        [
            gain_one, gain_two, shift_one, shift_two,
            half_to_full(sums[:, 0], OWN_HEADS, core), half_to_full(sums[:, 2], OWN_HEADS, core),
            out_bias, down_bias, upbias[0], upbias[1], upbias[2], upbias[3],
        ]
    )
    small = small + swap(small)
    small = jnp.pad(small.astype(BF).T, ((0, 0), (0, 8 * PIECE - 3 * FF_HALF - 12)))
    shares = lax.psum_scatter(
        jnp.concatenate([grad_qkv, grad_out, small], axis=1), "dp", scatter_dimension=0, tiled=True
    )
    rows = D // DP
    flat = jnp.concatenate([shares_up, shares_down[:rows], shares_down[rows:], shares], axis=1)
    pieces = flat.reshape(rows, CHIPS, PIECE).transpose(1, 0, 2)
    summed = jnp.sum(across_chips(pieces).astype(F32), axis=0).astype(BF)
    return grad_state, lax.all_gather(summed, "ctx", axis=0, tiled=False)


def unpack(whole):
    rows = D // DP
    halves = whole.reshape(CHIPS, CORES, rows, PIECE).transpose(1, 2, 0, 3)
    halves = halves.reshape(CORES, rows, CHIPS * PIECE).astype(F32)
    up, down_a, down_b, qkv, out, small = jnp.split(
        halves, [FF_HALF, FF_HALF + D, 2 * FF_HALF, 2 * FF_HALF + QKV_HALF, 3 * FF_HALF], axis=2
    )
    up = up.reshape(CORES, rows, DP, FF_PART).transpose(1, 2, 0, 3).reshape(rows, FF)
    down = jnp.stack([down_a, down_b], axis=1).reshape(FF // DP, D)
    qkv = qkv.reshape(CORES, rows, OWN_HEADS, 3, HEAD).transpose(1, 3, 2, 0, 4)
    qkv = qkv.reshape(rows, 3 * D)
    out = out.transpose(1, 0, 2).reshape(rows, D)
    small = small[0, :, :12].T
    return qkv, out, up, down, small[0:2], small[2:8], small[8:12].reshape(FF // DP)


def local(tokens, cotangent, w_qkv, w_out, w_up, w_down, gains, shifts, up_bias):
    core = lax.rem(lax.axis_index("ctx"), CORES)
    rows = D // DP

    def pick(value, axis):
        return lax.dynamic_index_in_dim(value, core, axis, keepdims=False)

    def gather(value, axis=0):
        return lax.all_gather(value, "dp", axis=axis, tiled=True)

    vectors = jnp.concatenate(
        [gains.reshape(-1, rows), shifts.reshape(-1, rows), up_bias.reshape(-1, rows)], axis=0
    )
    vectors = lax.all_gather(vectors, "dp", axis=0, tiled=False).transpose(1, 0, 2).astype(F32)
    all_gains = vectors[:4].reshape(LAYERS, 2, D)
    all_shifts = vectors[4:16].reshape(LAYERS, 6, D)
    all_up = vectors[16:24].reshape(LAYERS, CORES, 2, DP, FF_PART // 2).transpose(0, 1, 3, 2, 4)
    weights = []
    for layer in range(LAYERS):
        qkv_part = pick(w_qkv[layer].reshape(rows, 3, OWN_HEADS, CORES, HEAD), 3)
        qkv_part = qkv_part.transpose(0, 2, 1, 3).reshape(rows, QKV_HALF)
        first = gather(jnp.concatenate([qkv_part, w_out[layer]], axis=1))
        up = gather(pick(w_up[layer].reshape(rows, DP, CORES, FF_PART), 2).reshape(rows, FF_HALF))
        down = gather(pick(w_down[layer].reshape(CORES, FF_PART, D), 0))
        shift = all_shifts[layer]
        zeros = jnp.zeros((OWN_HEADS, HEAD), F32)
        qkv_bias = jnp.stack(
            [
                pick(shift[2].reshape(OWN_HEADS, CORES, HEAD), 1),
                zeros,
                pick(shift[3].reshape(OWN_HEADS, CORES, HEAD), 1),
            ],
            axis=1,
        ).reshape(QKV_HALF)
        bias = pick(all_up[layer], 0).reshape(FF_HALF)
        weights.append(
            (
                first[:, :QKV_HALF], first[:, QKV_HALF:], up, down,
                all_gains[layer], shift, qkv_bias, bias,
            )
        )
    state = tokens.astype(F32)
    saved = []
    for layer in range(LAYERS):
        state, kept = layer_forward(state, weights[layer], core)
        saved.append(kept)
    output = state.astype(BF)
    grad = cotangent.astype(F32)
    collected = [None] * LAYERS
    for layer in reversed(range(LAYERS)):
        grad, whole = layer_backward(saved[layer], weights[layer], grad, core)
        collected[layer] = unpack(whole)
    stacked = [jnp.stack([collected[layer][m] for layer in range(LAYERS)]) for m in range(7)]
    return (output, grad, *stacked)


def solution(mesh):
    placed = (
        P(("dp", "ctx"), None),
        P(("dp", "ctx"), None),
        P(None, "dp", None),
        P(None, "dp", None),
        P(None, "dp", None),
        P(None, "dp", None),
        P(None, None, "dp"),
        P(None, None, "dp"),
        P(None, "dp"),
    )
    return jax.shard_map(
        local,
        mesh=mesh,
        in_specs=placed,
        out_specs=placed,
        check_vma=False,
    )
```

```python
import jax
import jax.numpy as jnp
from jax import lax
from jax.experimental import pallas as pl
from jax.experimental.pallas import tpu as pltpu
from jax.sharding import PartitionSpec as P

HEADS = 12
HEAD = 64
LAYERS = 2
D = 768
FF = 3072
DP = 8
BLK = 128
CHIPS = 8
CORES = 2
PAIR = CORES * BLK
OWN_HEADS = HEADS // CORES
SEQ = CHIPS * PAIR
FF_PART = FF // DP // CORES
FF_HALF = FF // CORES
QKV_HALF = 3 * D // CORES
EPSILON = 1e-05
NEGATIVE = -1e30
SAME_CORE = [[CORES * u + k for u in range(CHIPS)] for k in range(CORES)]
OTHER_CORE = [(i, i ^ 1) for i in range(CHIPS * CORES)]
BF = jnp.bfloat16
F32 = jnp.float32


def dot(left, right, ldim, rdim):
    return lax.dot_general(
        left, right, (((ldim,), (rdim,)), ((), ())), preferred_element_type=F32
    )


def ring(axis, step, scale):
    size = 4
    count = 2 * size * scale
    moves = []
    for i in range(count):
        block, low = i // scale, i % scale
        pair, at = block // size, block % size
        moves.append((i, (pair * size + (at + step) % size) * scale + low))
    return lambda value: lax.ppermute(value, axis, moves)


def across(axis, scale):
    count = 8 * scale
    return lambda value: lax.ppermute(
        value, axis, [(i, (i + count // 2) % count) for i in range(count)]
    )


def places(axis, scale):
    block = lax.axis_index(axis) // scale
    pair, at = block // 4, block % 4
    return [[((pair + far) % 2) * 4 + (at + step) % 4 for step in range(4)] for far in range(2)]


def gather_start(value, axis, scale):
    value = value[None]
    far = across(axis, scale)(value)
    own_up, own_down = ring(axis, 1, scale)(value), ring(axis, -1, scale)(value)
    return value, far, own_up, own_down


def gather_go_on(begun, axis, scale, after_one=None, after_two=None):
    if after_one is not None:
        begun = tie(begun, after_one)[0]
    value, far, own_up, own_down = begun
    up, down = ring(axis, 1, scale), ring(axis, -1, scale)
    far_up, far_down = up(far), down(far)
    own_two = up(own_up)
    if after_two is not None:
        far_down = tie(far_down, after_two)[0]
    far_two = down(far_down)
    return value, own_up, own_two, own_down, far, far_up, far_two, far_down


def join_kernel(where_ref, *refs):
    pieces, parts = refs[:8], refs[8:]
    for k in range(8):
        at = 0
        for part in parts:
            rows = part.shape[1]
            part[where_ref[k]] = pieces[k][0, at : at + rows]
            at += rows


def gather_end(pieces, axis, scale, *heights):
    where = places(axis, scale)
    where = jnp.stack([where[k // 4][-(k % 4) % 4] for k in range(8)]).astype(jnp.int32)
    _, rows, width = pieces[0].shape
    return pl.pallas_call(
        join_kernel,
        in_specs=[pl.BlockSpec(memory_space=pltpu.SMEM)]
        + [pl.BlockSpec(memory_space=pltpu.VMEM)] * 8,
        out_shape=[
            jax.ShapeDtypeStruct((8, height, width), pieces[0].dtype) for height in heights or (rows,)
        ],
        compiler_params=pltpu.CompilerParams(vmem_limit_bytes=40 * 1024 * 1024),
        name="join",
    )(where, *pieces)


def ring_scatter(value, axis, scale, after):
    up, down, pair = ring(axis, 1, scale), ring(axis, -1, scale), across(axis, scale)
    where = places(axis, scale)
    value = value.reshape(8, value.shape[0] // 8, *value.shape[1:])

    def part(far, step):
        return lax.dynamic_index_in_dim(value, where[far][step], 0, keepdims=False)

    def add(*terms):
        total = terms[0].astype(F32)
        for term in terms[1:]:
            total = total + term.astype(F32)
        return total.astype(BF)

    own_two, far_two = up(part(0, 2)), down(part(1, 2))
    far_up, own_down = up(part(1, 1)), down(part(0, 3))
    own_two, far_two, far_up, own_down, after = tie(own_two, far_two, far_up, own_down, after)
    own_up = up(add(part(0, 1), own_two))
    far_down = down(add(part(1, 3), far_two))
    far = pair(add(part(1, 0), far_up, far_down))
    return add(part(0, 0), own_up, own_down, far), after


def tie(*values):
    return lax.optimization_barrier(values)


def swap(value):
    return lax.ppermute(value, "ctx", OTHER_CORE)


def diagonal_mask(size):
    key = lax.broadcasted_iota(jnp.int32, (size, size), 0)
    query = lax.broadcasted_iota(jnp.int32, (size, size), 1)
    return key <= query


def attend_kernel(qkv_ref, out_ref, ctx_ref, lse_ref):
    step = PAIR
    keys = [qkv_ref[j, HEAD : 2 * HEAD, :] for j in range(CHIPS)]
    allowed = diagonal_mask(step)
    for i in range(CHIPS):
        query = qkv_ref[i, 0:HEAD, :]
        scores = [dot(keys[j], query, 0, 0) for j in range(i + 1)]
        scores[i] = jnp.where(allowed, scores[i], NEGATIVE)
        peak = scores[0].max(axis=0, keepdims=True)
        for j in range(1, i + 1):
            peak = jnp.maximum(peak, scores[j].max(axis=0, keepdims=True))
        total = jnp.zeros((1, step), F32)
        accum = jnp.zeros((HEAD, step), F32)
        for j in range(i + 1):
            weights = jnp.exp(scores[j] - peak)
            total = total + weights.sum(axis=0, keepdims=True)
            accum = accum + dot(qkv_ref[j, 2 * HEAD : 3 * HEAD, :], weights.astype(BF), 1, 0)
        context = accum / total
        out_ref[2 * i] = context[:, :BLK].astype(BF)
        out_ref[2 * i + 1] = context[:, BLK:].astype(BF)
        ctx_ref[i] = context
        lse_ref[i] = peak + jnp.log(total)


def attend(qkv):
    return pl.pallas_call(
        attend_kernel,
        out_shape=(
            jax.ShapeDtypeStruct((CORES * CHIPS, HEAD, BLK), BF),
            jax.ShapeDtypeStruct((CHIPS, HEAD, PAIR), F32),
            jax.ShapeDtypeStruct((CHIPS, 1, PAIR), F32),
        ),
        compiler_params=pltpu.CompilerParams(vmem_limit_bytes=40 * 1024 * 1024),
        name="attend",
    )(qkv)


def attend_back_kernel(qkv_ref, grad_ref, ctx_ref, lse_ref, out_ref, dq_ref):
    allowed = diagonal_mask(PAIR)
    grads, deltas = [], []
    for i in range(CHIPS):
        grad = jnp.concatenate([grad_ref[2 * i], grad_ref[2 * i + 1]], axis=1)
        grads.append(grad)
        deltas.append((grad.astype(F32) * ctx_ref[i]).sum(axis=0, keepdims=True))
    for j in range(CHIPS):
        key = qkv_ref[j, HEAD : 2 * HEAD, :]
        value = qkv_ref[j, 2 * HEAD : 3 * HEAD, :]
        grad_key = jnp.zeros((HEAD, PAIR), F32)
        grad_value = jnp.zeros((HEAD, PAIR), F32)
        for i in range(j, CHIPS):
            query = qkv_ref[i, 0:HEAD, :]
            probs = jnp.exp(dot(key, query, 0, 0) - lse_ref[i])
            if i == j:
                probs = jnp.where(allowed, probs, 0.0)
            grad_probs = dot(value, grads[i], 0, 0)
            grad_scores = (probs * (grad_probs - deltas[i])).astype(BF)
            grad_value = grad_value + dot(grads[i], probs.astype(BF), 1, 1)
            grad_key = grad_key + dot(query, grad_scores, 1, 1)
            grad_query = dot(key, grad_scores, 1, 0)
            if j == 0:
                dq_ref[i] = grad_query
            else:
                dq_ref[i] = dq_ref[i] + grad_query
        out_ref[j, 0:HEAD, :] = (dq_ref[j] * HEAD**-0.5).astype(BF)
        out_ref[j, HEAD : 2 * HEAD, :] = grad_key.astype(BF)
        out_ref[j, 2 * HEAD : 3 * HEAD, :] = grad_value.astype(BF)


def attend_back(qkv, grad, context, logsum):
    return pl.pallas_call(
        attend_back_kernel,
        out_shape=jax.ShapeDtypeStruct((CHIPS, 3 * HEAD, PAIR), BF),
        scratch_shapes=[pltpu.VMEM((CHIPS, HEAD, PAIR), F32)],
        compiler_params=pltpu.CompilerParams(vmem_limit_bytes=40 * 1024 * 1024),
        name="attend_back",
    )(qkv, grad, context, logsum)


def norm_parts(values):
    average = jnp.mean(values, axis=-1, keepdims=True)
    centered = values - average
    spread = jnp.mean(centered * centered, axis=-1, keepdims=True)
    scale = lax.rsqrt(spread + EPSILON)
    return centered * scale, scale


def norm_back(grad, hat, scale, gain):
    scaled = grad * gain
    first = jnp.mean(scaled, axis=-1, keepdims=True)
    second = jnp.mean(scaled * hat, axis=-1, keepdims=True)
    part = scale * (scaled - first - hat * second)
    return part, jnp.sum(grad * hat, axis=0), jnp.sum(grad, axis=0)


def ordered(mine, other, core):
    three = jnp.concatenate([mine, other, mine], axis=0)
    return lax.dynamic_slice_in_dim(three, core * BLK, PAIR, 0)


def across_chips(value):
    return lax.all_to_all(value, "ctx", 0, 0, axis_index_groups=SAME_CORE, tiled=True)


def layer_forward(state, w_qkv, rest_part, vectors, core):
    gains, shifts, qkv_bias, up_bias = vectors
    hat_one, scale_one = norm_parts(state)
    mine = (hat_one * gains[0] + shifts[0]).astype(BF)
    normed = ordered(mine, swap(mine), core)
    rest = gather_start(rest_part, "dp", 1)
    mixed = (dot(w_qkv, normed, 0, 1) + qkv_bias[:, None]).reshape(OWN_HEADS, 3, HEAD, PAIR)
    factor = jnp.array([HEAD**-0.5, 1.0, 1.0], F32).reshape(1, 3, 1, 1)
    qkv = (mixed * factor).astype(BF).reshape(OWN_HEADS, 3 * HEAD, PAIR)
    qkv = jnp.concatenate([qkv, jnp.zeros((CHIPS - OWN_HEADS, 3 * HEAD, PAIR), BF)], axis=0)
    qkv = across_chips(qkv)
    out, context, logsum = attend(qkv)
    rest = gather_go_on(rest, "dp", 1, qkv, out)
    out = lax.all_to_all(out, "ctx", 0, 0, tiled=True)
    rest = gather_end(rest, "dp", 1)[0].reshape(D, -1)
    w_out, w_up, w_down = rest[:, :D], rest[:, D : D + FF_HALF], rest[:, D + FF_HALF : D + 2 * FF_HALF]
    attended = out[:HEADS].reshape(D, BLK)
    middle = state + (dot(attended, w_out, 0, 0) + shifts[4])
    hat_two, scale_two = norm_parts(middle)
    mine_two = (hat_two * gains[1] + shifts[1]).astype(BF)
    normed_two = jnp.concatenate([mine_two, swap(mine_two)], axis=0)
    upper = dot(normed_two, w_up, 1, 0) + up_bias
    active = jax.nn.gelu(upper).astype(BF)
    partial = dot(active[:, :D], w_down[:, :D], 1, 0) + dot(active[:, D:], w_down[:, D:], 1, 0)
    result = middle + (partial[:BLK] + swap(partial[BLK:].astype(BF)).astype(F32) + shifts[5])
    kept = (
        hat_one, scale_one, normed, qkv, context, logsum,
        attended, hat_two, scale_two, normed_two, upper, active,
    )
    weights = (w_qkv, w_out, w_up, w_down, gains)
    return result, kept, weights, rest


def half_to_full(vector, parts, core):
    piece = vector.reshape(parts, 1, -1)
    slot = lax.broadcasted_iota(jnp.int32, (parts, CORES, piece.shape[2]), 1)
    return jnp.where(slot == core, piece, 0.0).reshape(-1)


def layer_backward(kept, weights, grad_result, core, earlier):
    (
        hat_one, scale_one, normed, qkv, context, logsum,
        attended, hat_two, scale_two, normed_two, upper, active,
    ) = kept
    w_qkv, w_out, w_up, w_down, gains = weights
    mine = grad_result.astype(BF)
    down_bias = jnp.sum(mine.astype(F32), axis=0)
    both = jnp.concatenate([mine, swap(mine)], axis=0)
    grad_active = jnp.concatenate(
        [dot(both, w_down[:, :D], 1, 1), dot(both, w_down[:, D:], 1, 1)], axis=1
    )
    gelu_back = jax.vjp(jax.nn.gelu, upper)[1]
    grad_upper = gelu_back(grad_active)[0].astype(BF)
    partial = dot(grad_upper, w_up, 1, 1)
    grad_normed_two = partial[:BLK] + swap(partial[BLK:].astype(BF)).astype(F32)
    grad_down = dot(active, both, 0, 0).astype(BF)
    grad_up = dot(normed_two, grad_upper, 0, 0).astype(BF)
    grad_upbias = jnp.sum(grad_upper.astype(F32), axis=0)
    part, gain_two, shift_two = norm_back(grad_normed_two, hat_two, scale_two, gains[1])
    grad_middle = grad_result + part
    branch = grad_middle.astype(BF)
    out_bias = jnp.sum(branch.astype(F32), axis=0)
    grad_out_t = dot(w_out, branch, 1, 1).astype(BF).reshape(HEADS, HEAD, BLK)
    grad_out_t = jnp.concatenate(
        [grad_out_t, jnp.zeros((CHIPS * CORES - HEADS, HEAD, BLK), BF)], axis=0
    )
    grad_context = lax.all_to_all(grad_out_t, "ctx", 0, 0, tiled=True)
    grad_out = dot(attended, branch, 1, 0)
    columns = D // CORES
    keep = lax.dynamic_slice_in_dim(grad_out, core * columns, columns, 1)
    give = lax.dynamic_slice_in_dim(grad_out, (1 - core) * columns, columns, 1)
    grad_out = (keep + swap(give.astype(BF)).astype(F32)).astype(BF)
    wide = jnp.concatenate([grad_up, grad_down[:D], grad_down[D:], grad_out], axis=1)
    grad_context, wide = tie(grad_context, wide)
    shares = lax.psum_scatter(wide, "dp", scatter_dimension=0, tiled=True)
    if earlier is not None:
        grad_context, earlier = tie(grad_context, earlier)
        earlier = chip_sum(earlier, 4096)
    grad_mixed = attend_back(qkv, grad_context, context, logsum)
    if earlier is not None:
        grad_mixed, earlier = tie(grad_mixed, earlier)
    grad_mixed = across_chips(grad_mixed)
    grad_mixed = grad_mixed[:OWN_HEADS].reshape(QKV_HALF, PAIR)
    partial = dot(grad_mixed, w_qkv, 0, 1)
    mine = lax.dynamic_slice_in_dim(partial, core * BLK, BLK, 0)
    other = lax.dynamic_slice_in_dim(partial, (1 - core) * BLK, BLK, 0)
    grad_normed = mine + swap(other.astype(BF)).astype(F32)
    grad_qkv = dot(normed, grad_mixed, 0, 1).astype(BF)
    sums = jnp.sum(grad_mixed.astype(F32), axis=1).reshape(OWN_HEADS, 3, HEAD)
    part, gain_one, shift_one = norm_back(grad_normed, hat_one, scale_one, gains[0])
    grad_state = grad_middle + part
    upbias = grad_upbias.reshape(2, D)
    empty = jnp.zeros_like(upbias)
    upbias = jnp.concatenate(
        [jnp.where(core == 0, upbias, empty), jnp.where(core == 1, upbias, empty)], axis=0
    )
    small = jnp.stack(
        [
            gain_one, gain_two, shift_one, shift_two,
            half_to_full(sums[:, 0], OWN_HEADS, core), half_to_full(sums[:, 2], OWN_HEADS, core),
            out_bias, down_bias, upbias[0], upbias[1], upbias[2], upbias[3],
        ]
    )
    small = small + swap(small)
    small = jnp.pad(small.astype(BF).T, ((0, 0), (0, 128 - 12)))
    grad_rest = jnp.concatenate([grad_qkv, small], axis=1)
    if earlier is None:
        grad_state, grad_rest = tie(grad_state, grad_rest)
    return grad_state, shares, grad_rest, earlier


def chip_sum(shares, width):
    rows = D // DP
    shares = jnp.pad(shares, ((0, 0), (0, width - shares.shape[1])))
    pieces = shares.reshape(rows, CHIPS, width // CHIPS).transpose(1, 0, 2)
    moved = lax.all_to_all(pieces, "ctx", 0, 0, axis_index_groups=SAME_CORE, tiled=True)
    return jnp.sum(moved.astype(F32), axis=0).astype(BF)


def to_all_chips(summed):
    mine = gather_go_on(gather_start(summed, "ctx", CORES), "ctx", CORES)
    mine = gather_end(mine, "ctx", CORES)[0]
    return mine, swap(mine)


def unpack_kernel(core_ref, *refs):
    pairs, (qkv_ref, out_ref, up_ref, down_ref, small_ref, flat) = refs[:4], refs[4:]
    rows = D // DP

    @pl.when(pl.program_id(0) == 0)
    def _():
        first = core_ref[0] == 0
        at = 0
        for mine_ref, other_ref in (pairs[:2], pairs[2:]):
            size = mine_ref.shape[2]
            for c in range(CHIPS):
                mine, other = mine_ref[c].astype(F32), other_ref[c].astype(F32)
                flat[0, :, at : at + size] = jnp.where(first, mine, other)
                flat[1, :, at : at + size] = jnp.where(first, other, mine)
                at += size

    def layer(mlp, rest):
        def part(k, start, size):
            low, high = start // 128 * 128, -(-(start + size) // 128) * 128
            return flat[k, :, low:high][:, start - low : start - low + size]

        for d in range(DP):
            pieces = [
                part(k, mlp + e * D + d * rows, rows) for k in range(CORES) for e in range(2)
            ]
            up_ref[0, :, d * 4 * rows : (d + 1) * 4 * rows] = jnp.concatenate(pieces, axis=1)
        for k in range(CORES):
            for e in range(2):
                at = mlp + FF_HALF + e * D
                down_ref[0, (2 * k + e) * rows : (2 * k + e + 1) * rows, :] = flat[k, :, at : at + D]
            at = mlp + 2 * FF_HALF
            out_ref[0, :, k * D // 2 : (k + 1) * D // 2] = flat[k, :, at : at + D // 2]
        for t in range(3):
            for u in range(OWN_HEADS):
                pieces = [part(k, rest + (u * 3 + t) * HEAD, HEAD) for k in range(CORES)]
                to = t * D + u * 2 * HEAD
                qkv_ref[0, :, to : to + 2 * HEAD] = jnp.concatenate(pieces, axis=1)
        small_ref[0] = flat[0, :, rest + QKV_HALF : rest + QKV_HALF + 128].T[:16]

    late = 4096 + 2 * FF_HALF + D // 2
    pl.when(pl.program_id(0) == 0)(lambda: layer(4096, late + QKV_HALF + 128))
    pl.when(pl.program_id(0) == 1)(lambda: layer(0, late))


def unpack(core, *pairs):
    rows = D // DP
    shapes = [(rows, 3 * D), (rows, D), (rows, FF), (FF // DP, D), (16, rows)]
    return pl.pallas_call(
        unpack_kernel,
        grid=(LAYERS,),
        in_specs=[pl.BlockSpec(memory_space=pltpu.SMEM)]
        + [pl.BlockSpec(pair.shape, lambda i: (0, 0, 0)) for pair in pairs],
        out_specs=[pl.BlockSpec((1, *shape), lambda i: (i, 0, 0)) for shape in shapes],
        out_shape=[jax.ShapeDtypeStruct((LAYERS, *shape), F32) for shape in shapes],
        scratch_shapes=[pltpu.VMEM((CORES, rows, 4096 + 6144), F32)],
        compiler_params=pltpu.CompilerParams(vmem_limit_bytes=48 * 1024 * 1024),
        name="unpack",
    )(core.reshape(1), *pairs)


def local(tokens, cotangent, w_qkv, w_out, w_up, w_down, gains, shifts, up_bias):
    core = lax.rem(lax.axis_index("ctx"), CORES)
    rows = D // DP

    def pick(value, axis):
        return lax.dynamic_index_in_dim(value, core, axis, keepdims=False)

    vectors = jnp.concatenate(
        [gains.reshape(-1, rows), shifts.reshape(-1, rows), up_bias.reshape(-1, rows)], axis=0
    )
    vectors = jnp.pad(vectors.reshape(2, QKV_HALF), ((0, 14), (0, 0)))
    weights = []
    qkv_parts, rest_parts = [], []
    for layer in range(LAYERS):
        qkv_part = pick(w_qkv[layer].reshape(rows, 3, OWN_HEADS, CORES, HEAD), 3)
        qkv_parts.append(qkv_part.transpose(0, 2, 1, 3).reshape(rows, QKV_HALF))
        up = pick(w_up[layer].reshape(rows, DP, CORES, 2, rows), 2)
        up = up.transpose(0, 2, 1, 3).reshape(rows, FF_HALF)
        down = pick(w_down[layer].reshape(CORES, 2, rows, D), 0)
        rest_parts.append([w_out[layer], up, down[0], down[1]])
    first = gather_start(jnp.concatenate([qkv_parts[0], vectors], axis=0), "dp", 1)
    first, vectors = gather_end(gather_go_on(first, "dp", 1), "dp", 1, rows, 16)
    vectors = vectors[:, :2].reshape(DP, 24, rows).transpose(1, 0, 2).astype(F32)
    all_gains = vectors[:4].reshape(LAYERS, 2, D)
    all_shifts = vectors[4:16].reshape(LAYERS, 6, D)
    all_up = vectors[16:24].reshape(LAYERS, CORES, 2, DP, rows)
    w_now = first.reshape(D, QKV_HALF)
    rest_part = jnp.concatenate([*rest_parts[0], qkv_parts[1]], axis=1)
    rest_part = tie(rest_part, w_now)[0]
    state = tokens.astype(F32)
    saved = []
    for layer in range(LAYERS):
        shift = all_shifts[layer]
        zeros = jnp.zeros((OWN_HEADS, HEAD), F32)
        qkv_bias = jnp.stack(
            [
                pick(shift[2].reshape(OWN_HEADS, CORES, HEAD), 1),
                zeros,
                pick(shift[3].reshape(OWN_HEADS, CORES, HEAD), 1),
            ],
            axis=1,
        ).reshape(QKV_HALF)
        bias = pick(all_up[layer], 0).reshape(FF_HALF)
        few = (all_gains[layer], shift, qkv_bias, bias)
        state, kept, weights, rest = layer_forward(state, w_now, rest_part, few, core)
        if layer + 1 < LAYERS:
            w_now = rest[:, D + 2 * FF_HALF :]
            rest_part = jnp.concatenate(rest_parts[1], axis=1)
            rest_part = tie(rest_part, rest)[0]
        saved.append((kept, weights))
    output = state.astype(BF)
    grad = cotangent.astype(F32)
    grad, shares_one, rest_one, _ = layer_backward(*saved[1], grad, core, None)
    grad, shares_two, rest_two, early = layer_backward(*saved[0], grad, core, shares_one)
    rest = jnp.concatenate([rest_one, rest_two], axis=1)
    rest, early = ring_scatter(rest, "dp", 1, early)
    early = to_all_chips(early)
    late = jnp.concatenate([shares_two, rest], axis=1)
    late = to_all_chips(chip_sum(late, 6144))
    grad_qkv, grad_out, grad_up, grad_down, small = unpack(core, *early, *late)
    return (
        output, grad, grad_qkv, grad_out, grad_up, grad_down,
        small[:, 0:2], small[:, 2:8], small[:, 8:12].reshape(LAYERS, FF // DP),
    )


def solution(mesh):
    placed = (
        P(("dp", "ctx"), None),
        P(("dp", "ctx"), None),
        P(None, "dp", None),
        P(None, "dp", None),
        P(None, "dp", None),
        P(None, "dp", None),
        P(None, None, "dp"),
        P(None, None, "dp"),
        P(None, "dp"),
    )
    return jax.shard_map(
        local,
        mesh=mesh,
        in_specs=placed,
        out_specs=placed,
        check_vma=False,
    )
```

```python
import jax
import jax.numpy as jnp
from jax import lax
from jax.experimental import pallas as pl
from jax.experimental.pallas import tpu as pltpu
from jax.sharding import PartitionSpec as P

HEADS = 12
HEAD = 64
LAYERS = 2
D = 768
FF = 3072
DP = 8
BLK = 128
CHIPS = 8
CORES = 2
PAIR = CORES * BLK
OWN_HEADS = HEADS // CORES
SEQ = CHIPS * PAIR
FF_PART = FF // DP // CORES
FF_HALF = FF // CORES
QKV_HALF = 3 * D // CORES
EPSILON = 1e-05
NEGATIVE = -1e30
EARLY = 4096
LATE = 6144
SAME_CORE = [[CORES * u + k for u in range(CHIPS)] for k in range(CORES)]
OTHER_CORE = [(i, i ^ 1) for i in range(CHIPS * CORES)]
BF = jnp.bfloat16
F32 = jnp.float32


def dot(left, right, ldim, rdim):
    return lax.dot_general(
        left, right, (((ldim,), (rdim,)), ((), ())), preferred_element_type=F32
    )


def ring(axis, step, scale):
    size = 4
    count = 2 * size * scale
    moves = []
    for i in range(count):
        block, low = i // scale, i % scale
        pair, at = block // size, block % size
        moves.append((i, (pair * size + (at + step) % size) * scale + low))
    return lambda value: lax.ppermute(value, axis, moves)


def across(axis, scale):
    count = 8 * scale
    return lambda value: lax.ppermute(
        value, axis, [(i, (i + count // 2) % count) for i in range(count)]
    )


def places(axis, scale):
    block = lax.axis_index(axis) // scale
    pair, at = block // 4, block % 4
    return [[((pair + far) % 2) * 4 + (at + step) % 4 for step in range(4)] for far in range(2)]


def gather_start(value, axis, scale):
    value = value[None]
    far = across(axis, scale)(value)
    own_up, own_down = ring(axis, 1, scale)(value), ring(axis, -1, scale)(value)
    return value, far, own_up, own_down


def gather_go_on(begun, axis, scale, after_one=None, after_two=None):
    if after_one is not None:
        begun = tie(begun, after_one)[0]
    value, far, own_up, own_down = begun
    up, down = ring(axis, 1, scale), ring(axis, -1, scale)
    far_up, far_down = up(far), down(far)
    own_two = up(own_up)
    if after_two is not None:
        far_down = tie(far_down, after_two)[0]
    far_two = down(far_down)
    return value, own_up, own_two, own_down, far, far_up, far_two, far_down


def join_kernel(where_ref, *refs):
    pieces, parts = refs[:8], refs[8:]
    for k in range(8):
        at = 0
        for part in parts:
            rows = part.shape[1]
            part[where_ref[k]] = pieces[k][0, at : at + rows]
            at += rows


def gather_end(pieces, axis, scale, *heights):
    where = places(axis, scale)
    where = jnp.stack([where[k // 4][-(k % 4) % 4] for k in range(8)]).astype(jnp.int32)
    _, rows, width = pieces[0].shape
    return pl.pallas_call(
        join_kernel,
        in_specs=[pl.BlockSpec(memory_space=pltpu.SMEM)]
        + [pl.BlockSpec(memory_space=pltpu.VMEM)] * 8,
        out_shape=[
            jax.ShapeDtypeStruct((8, height, width), pieces[0].dtype) for height in heights or (rows,)
        ],
        compiler_params=pltpu.CompilerParams(vmem_limit_bytes=40 * 1024 * 1024),
        name="join",
    )(where, *pieces)


def ring_scatter(value, axis, scale):
    up, down, pair = ring(axis, 1, scale), ring(axis, -1, scale), across(axis, scale)
    where = places(axis, scale)
    value = value.reshape(8, value.shape[0] // 8, *value.shape[1:])

    def part(far, step):
        return lax.dynamic_index_in_dim(value, where[far][step], 0, keepdims=False)

    def add(*terms):
        total = terms[0].astype(F32)
        for term in terms[1:]:
            total = total + term.astype(F32)
        return total.astype(BF)

    own_two, far_two = up(part(0, 2)), down(part(1, 2))
    far_up, own_down = up(part(1, 1)), down(part(0, 3))
    own_up = up(add(part(0, 1), own_two))
    far_down = down(add(part(1, 3), far_two))
    far = pair(add(part(1, 0), far_up, far_down))
    return add(part(0, 0), own_up, own_down, far)


def tie(*values):
    return lax.optimization_barrier(values)


def swap(value):
    return lax.ppermute(value, "ctx", OTHER_CORE)


def diagonal_mask(size):
    key = lax.broadcasted_iota(jnp.int32, (size, size), 0)
    query = lax.broadcasted_iota(jnp.int32, (size, size), 1)
    return key <= query


def attend_kernel(qkv_ref, out_ref, ctx_ref, lse_ref):
    step = PAIR
    keys = [qkv_ref[j, HEAD : 2 * HEAD, :] for j in range(CHIPS)]
    allowed = diagonal_mask(step)
    for i in range(CHIPS):
        query = qkv_ref[i, 0:HEAD, :]
        scores = [dot(keys[j], query, 0, 0) for j in range(i + 1)]
        scores[i] = jnp.where(allowed, scores[i], NEGATIVE)
        peak = scores[0].max(axis=0, keepdims=True)
        for j in range(1, i + 1):
            peak = jnp.maximum(peak, scores[j].max(axis=0, keepdims=True))
        total = jnp.zeros((1, step), F32)
        accum = jnp.zeros((HEAD, step), F32)
        for j in range(i + 1):
            weights = jnp.exp(scores[j] - peak)
            total = total + weights.sum(axis=0, keepdims=True)
            accum = accum + dot(qkv_ref[j, 2 * HEAD : 3 * HEAD, :], weights.astype(BF), 1, 0)
        context = accum / total
        out_ref[2 * i] = context[:, :BLK].astype(BF)
        out_ref[2 * i + 1] = context[:, BLK:].astype(BF)
        ctx_ref[i] = context
        lse_ref[i] = peak + jnp.log(total)


def attend(qkv):
    return pl.pallas_call(
        attend_kernel,
        out_shape=(
            jax.ShapeDtypeStruct((CORES * CHIPS, HEAD, BLK), BF),
            jax.ShapeDtypeStruct((CHIPS, HEAD, PAIR), F32),
            jax.ShapeDtypeStruct((CHIPS, 1, PAIR), F32),
        ),
        compiler_params=pltpu.CompilerParams(vmem_limit_bytes=40 * 1024 * 1024),
        name="attend",
    )(qkv)


def attend_back_kernel(qkv_ref, grad_ref, ctx_ref, lse_ref, out_ref, dq_ref):
    allowed = diagonal_mask(PAIR)
    grads, deltas = [], []
    for i in range(CHIPS):
        grad = jnp.concatenate([grad_ref[2 * i], grad_ref[2 * i + 1]], axis=1)
        grads.append(grad)
        deltas.append((grad.astype(F32) * ctx_ref[i]).sum(axis=0, keepdims=True))
    for j in range(CHIPS):
        key = qkv_ref[j, HEAD : 2 * HEAD, :]
        value = qkv_ref[j, 2 * HEAD : 3 * HEAD, :]
        grad_key = jnp.zeros((HEAD, PAIR), F32)
        grad_value = jnp.zeros((HEAD, PAIR), F32)
        for i in range(j, CHIPS):
            query = qkv_ref[i, 0:HEAD, :]
            probs = jnp.exp(dot(key, query, 0, 0) - lse_ref[i])
            if i == j:
                probs = jnp.where(allowed, probs, 0.0)
            grad_probs = dot(value, grads[i], 0, 0)
            grad_scores = (probs * (grad_probs - deltas[i])).astype(BF)
            grad_value = grad_value + dot(grads[i], probs.astype(BF), 1, 1)
            grad_key = grad_key + dot(query, grad_scores, 1, 1)
            grad_query = dot(key, grad_scores, 1, 0)
            if j == 0:
                dq_ref[i] = grad_query
            else:
                dq_ref[i] = dq_ref[i] + grad_query
        out_ref[j, 0:HEAD, :] = (dq_ref[j] * HEAD**-0.5).astype(BF)
        out_ref[j, HEAD : 2 * HEAD, :] = grad_key.astype(BF)
        out_ref[j, 2 * HEAD : 3 * HEAD, :] = grad_value.astype(BF)


def attend_back(qkv, grad, context, logsum):
    return pl.pallas_call(
        attend_back_kernel,
        out_shape=jax.ShapeDtypeStruct((CHIPS, 3 * HEAD, PAIR), BF),
        scratch_shapes=[pltpu.VMEM((CHIPS, HEAD, PAIR), F32)],
        compiler_params=pltpu.CompilerParams(vmem_limit_bytes=40 * 1024 * 1024),
        name="attend_back",
    )(qkv, grad, context, logsum)


def norm_parts(values):
    average = jnp.mean(values, axis=-1, keepdims=True)
    centered = values - average
    spread = jnp.mean(centered * centered, axis=-1, keepdims=True)
    scale = lax.rsqrt(spread + EPSILON)
    return centered * scale, scale


def norm_back(grad, hat, scale, gain):
    scaled = grad * gain
    first = jnp.mean(scaled, axis=-1, keepdims=True)
    second = jnp.mean(scaled * hat, axis=-1, keepdims=True)
    part = scale * (scaled - first - hat * second)
    return part, jnp.sum(grad * hat, axis=0), jnp.sum(grad, axis=0)


def ordered(mine, other, core):
    three = jnp.concatenate([mine, other, mine], axis=0)
    return lax.dynamic_slice_in_dim(three, core * BLK, PAIR, 0)


def across_chips(value):
    return lax.all_to_all(value, "ctx", 0, 0, axis_index_groups=SAME_CORE, tiled=True)


def layer_forward(state, w_qkv, rest_part, vectors, core):
    gains, shifts, qkv_bias, up_bias = vectors
    hat_one, scale_one = norm_parts(state)
    mine = (hat_one * gains[0] + shifts[0]).astype(BF)
    normed = ordered(mine, swap(mine), core)
    rest = gather_start(rest_part, "dp", 1)
    mixed = (dot(w_qkv, normed, 0, 1) + qkv_bias[:, None]).reshape(OWN_HEADS, 3, HEAD, PAIR)
    factor = jnp.array([HEAD**-0.5, 1.0, 1.0], F32).reshape(1, 3, 1, 1)
    qkv = (mixed * factor).astype(BF).reshape(OWN_HEADS, 3 * HEAD, PAIR)
    qkv = jnp.concatenate([qkv, jnp.zeros((CHIPS - OWN_HEADS, 3 * HEAD, PAIR), BF)], axis=0)
    qkv = across_chips(qkv)
    out, context, logsum = attend(qkv)
    rest = gather_go_on(rest, "dp", 1, qkv, out)
    out = lax.all_to_all(out, "ctx", 0, 0, tiled=True)
    rest = gather_end(rest, "dp", 1)[0].reshape(D, -1)
    w_out, w_up, w_down = rest[:, :D], rest[:, D : D + FF_HALF], rest[:, D + FF_HALF : D + 2 * FF_HALF]
    attended = out[:HEADS].reshape(D, BLK)
    middle = state + (dot(attended, w_out, 0, 0) + shifts[4])
    hat_two, scale_two = norm_parts(middle)
    mine_two = (hat_two * gains[1] + shifts[1]).astype(BF)
    normed_two = jnp.concatenate([mine_two, swap(mine_two)], axis=0)
    upper = dot(normed_two, w_up, 1, 0) + up_bias
    active = jax.nn.gelu(upper).astype(BF)
    partial = dot(active[:, :D], w_down[:, :D], 1, 0) + dot(active[:, D:], w_down[:, D:], 1, 0)
    result = middle + (partial[:BLK] + swap(partial[BLK:].astype(BF)).astype(F32) + shifts[5])
    kept = (
        hat_one, scale_one, normed, qkv, context, logsum,
        attended, hat_two, scale_two, normed_two, upper, active,
    )
    weights = (w_qkv, w_out, w_up, w_down, gains)
    return result, kept, weights, rest


def half_to_full(vector, parts, core):
    piece = vector.reshape(parts, 1, -1)
    slot = lax.broadcasted_iota(jnp.int32, (parts, CORES, piece.shape[2]), 1)
    return jnp.where(slot == core, piece, 0.0).reshape(-1)


def layer_backward(kept, weights, grad_result, core, earlier):
    (
        hat_one, scale_one, normed, qkv, context, logsum,
        attended, hat_two, scale_two, normed_two, upper, active,
    ) = kept
    w_qkv, w_out, w_up, w_down, gains = weights
    mine = grad_result.astype(BF)
    down_bias = jnp.sum(mine.astype(F32), axis=0)
    both = jnp.concatenate([mine, swap(mine)], axis=0)
    grad_active = jnp.concatenate(
        [dot(both, w_down[:, :D], 1, 1), dot(both, w_down[:, D:], 1, 1)], axis=1
    )
    gelu_back = jax.vjp(jax.nn.gelu, upper)[1]
    grad_upper = gelu_back(grad_active)[0].astype(BF)
    partial = dot(grad_upper, w_up, 1, 1)
    grad_normed_two = partial[:BLK] + swap(partial[BLK:].astype(BF)).astype(F32)
    grad_down = dot(active, both, 0, 0).astype(BF)
    grad_up = dot(normed_two, grad_upper, 0, 0).astype(BF)
    grad_upbias = jnp.sum(grad_upper.astype(F32), axis=0)
    part, gain_two, shift_two = norm_back(grad_normed_two, hat_two, scale_two, gains[1])
    grad_middle = grad_result + part
    branch = grad_middle.astype(BF)
    out_bias = jnp.sum(branch.astype(F32), axis=0)
    grad_out_t = dot(w_out, branch, 1, 1).astype(BF).reshape(HEADS, HEAD, BLK)
    grad_out_t = jnp.concatenate(
        [grad_out_t, jnp.zeros((CHIPS * CORES - HEADS, HEAD, BLK), BF)], axis=0
    )
    grad_context = lax.all_to_all(grad_out_t, "ctx", 0, 0, tiled=True)
    grad_out = dot(attended, branch, 1, 0)
    columns = D // CORES
    keep = lax.dynamic_slice_in_dim(grad_out, core * columns, columns, 1)
    give = lax.dynamic_slice_in_dim(grad_out, (1 - core) * columns, columns, 1)
    grad_out = (keep + swap(give.astype(BF)).astype(F32)).astype(BF)
    wide = jnp.concatenate([grad_up, grad_down[:D], grad_down[D:], grad_out], axis=1)
    grad_context, wide = tie(grad_context, wide)
    shares = lax.psum_scatter(wide, "dp", scatter_dimension=0, tiled=True)
    if earlier is not None:
        grad_context, earlier = tie(grad_context, earlier)
        earlier = chip_sum(earlier, EARLY)
    grad_mixed = attend_back(qkv, grad_context, context, logsum)
    if earlier is not None:
        grad_mixed, earlier = tie(grad_mixed, earlier)
    grad_mixed = across_chips(grad_mixed)
    grad_mixed = grad_mixed[:OWN_HEADS].reshape(QKV_HALF, PAIR)
    partial = dot(grad_mixed, w_qkv, 0, 1)
    mine = lax.dynamic_slice_in_dim(partial, core * BLK, BLK, 0)
    other = lax.dynamic_slice_in_dim(partial, (1 - core) * BLK, BLK, 0)
    grad_normed = mine + swap(other.astype(BF)).astype(F32)
    grad_qkv = dot(normed, grad_mixed, 0, 1).astype(BF)
    sums = jnp.sum(grad_mixed.astype(F32), axis=1).reshape(OWN_HEADS, 3, HEAD)
    part, gain_one, shift_one = norm_back(grad_normed, hat_one, scale_one, gains[0])
    grad_state = grad_middle + part
    upbias = grad_upbias.reshape(2, D)
    empty = jnp.zeros_like(upbias)
    upbias = jnp.concatenate(
        [jnp.where(core == 0, upbias, empty), jnp.where(core == 1, upbias, empty)], axis=0
    )
    small = jnp.stack(
        [
            gain_one, gain_two, shift_one, shift_two,
            half_to_full(sums[:, 0], OWN_HEADS, core), half_to_full(sums[:, 2], OWN_HEADS, core),
            out_bias, down_bias, upbias[0], upbias[1], upbias[2], upbias[3],
        ]
    )
    small = small + swap(small)
    small = jnp.pad(small.astype(BF).T, ((0, 0), (0, 128 - 12)))
    grad_rest = jnp.concatenate([grad_qkv, small], axis=1)
    if earlier is None:
        grad_state, grad_rest = tie(grad_state, grad_rest)
    return grad_state, shares, grad_rest, earlier


def chip_sum(shares, width):
    rows = D // DP
    shares = jnp.pad(shares, ((0, 0), (0, width - shares.shape[1])))
    pieces = shares.reshape(rows, CHIPS, width // CHIPS).transpose(1, 0, 2)
    moved = lax.all_to_all(pieces, "ctx", 0, 0, axis_index_groups=SAME_CORE, tiled=True)
    return jnp.sum(moved.astype(F32), axis=0).astype(BF)


def to_all_chips(summed):
    mine = gather_go_on(gather_start(summed, "ctx", CORES), "ctx", CORES)
    mine = gather_end(mine, "ctx", CORES)[0]
    return mine, swap(mine)


def unpack_kernel(core_ref, *refs):
    mine_ref, other_ref, qkv_ref, out_ref, up_ref, down_ref, small_ref, flat = refs
    rows = D // DP

    @pl.when(pl.program_id(0) == 0)
    def _():
        first = core_ref[0] == 0
        at = 0
        for start, size in ((0, EARLY // CHIPS), (EARLY // CHIPS, LATE // CHIPS)):
            for c in range(CHIPS):
                mine = mine_ref[c, :, start : start + size].astype(F32)
                other = other_ref[c, :, start : start + size].astype(F32)
                flat[0, :, at : at + size] = jnp.where(first, mine, other)
                flat[1, :, at : at + size] = jnp.where(first, other, mine)
                at += size

    def layer(mlp, rest):
        def part(k, start, size):
            low, high = start // 128 * 128, -(-(start + size) // 128) * 128
            return flat[k, :, low:high][:, start - low : start - low + size]

        for d in range(DP):
            pieces = [
                part(k, mlp + e * D + d * rows, rows) for k in range(CORES) for e in range(2)
            ]
            up_ref[0, :, d * 4 * rows : (d + 1) * 4 * rows] = jnp.concatenate(pieces, axis=1)
        for k in range(CORES):
            for e in range(2):
                at = mlp + FF_HALF + e * D
                down_ref[0, (2 * k + e) * rows : (2 * k + e + 1) * rows, :] = flat[k, :, at : at + D]
            at = mlp + 2 * FF_HALF
            out_ref[0, :, k * D // 2 : (k + 1) * D // 2] = flat[k, :, at : at + D // 2]
        for t in range(3):
            for u in range(OWN_HEADS):
                pieces = [part(k, rest + (u * 3 + t) * HEAD, HEAD) for k in range(CORES)]
                to = t * D + u * 2 * HEAD
                qkv_ref[0, :, to : to + 2 * HEAD] = jnp.concatenate(pieces, axis=1)
        small_ref[0] = flat[0, :, rest + QKV_HALF : rest + QKV_HALF + 128].T[:16]

    late = EARLY + 2 * FF_HALF + D // 2
    pl.when(pl.program_id(0) == 0)(lambda: layer(EARLY, late + QKV_HALF + 128))
    pl.when(pl.program_id(0) == 1)(lambda: layer(0, late))


def unpack(core, *pairs):
    rows = D // DP
    shapes = [(rows, 3 * D), (rows, D), (rows, FF), (FF // DP, D), (16, rows)]
    return pl.pallas_call(
        unpack_kernel,
        grid=(LAYERS,),
        in_specs=[pl.BlockSpec(memory_space=pltpu.SMEM)]
        + [pl.BlockSpec(pair.shape, lambda i: (0, 0, 0)) for pair in pairs],
        out_specs=[pl.BlockSpec((1, *shape), lambda i: (i, 0, 0)) for shape in shapes],
        out_shape=[jax.ShapeDtypeStruct((LAYERS, *shape), F32) for shape in shapes],
        scratch_shapes=[pltpu.VMEM((CORES, rows, EARLY + LATE), F32)],
        compiler_params=pltpu.CompilerParams(vmem_limit_bytes=48 * 1024 * 1024),
        name="unpack",
    )(core.reshape(1), *pairs)


def local(tokens, cotangent, w_qkv, w_out, w_up, w_down, gains, shifts, up_bias):
    core = lax.rem(lax.axis_index("ctx"), CORES)
    rows = D // DP

    def pick(value, axis):
        return lax.dynamic_index_in_dim(value, core, axis, keepdims=False)

    vectors = jnp.concatenate(
        [gains.reshape(-1, rows), shifts.reshape(-1, rows), up_bias.reshape(-1, rows)], axis=0
    )
    vectors = jnp.pad(vectors.reshape(2, QKV_HALF), ((0, 14), (0, 0)))
    weights = []
    qkv_parts, rest_parts = [], []
    for layer in range(LAYERS):
        qkv_part = pick(w_qkv[layer].reshape(rows, 3, OWN_HEADS, CORES, HEAD), 3)
        qkv_parts.append(qkv_part.transpose(0, 2, 1, 3).reshape(rows, QKV_HALF))
        up = pick(w_up[layer].reshape(rows, DP, CORES, 2, rows), 2)
        up = up.transpose(0, 2, 1, 3).reshape(rows, FF_HALF)
        down = pick(w_down[layer].reshape(CORES, 2, rows, D), 0)
        rest_parts.append([w_out[layer], up, down[0], down[1]])
    first = gather_start(jnp.concatenate([qkv_parts[0], vectors], axis=0), "dp", 1)
    first, vectors = gather_end(gather_go_on(first, "dp", 1), "dp", 1, rows, 16)
    vectors = vectors[:, :2].reshape(DP, 24, rows).transpose(1, 0, 2).astype(F32)
    all_gains = vectors[:4].reshape(LAYERS, 2, D)
    all_shifts = vectors[4:16].reshape(LAYERS, 6, D)
    all_up = vectors[16:24].reshape(LAYERS, CORES, 2, DP, rows)
    w_now = first.reshape(D, QKV_HALF)
    rest_part = jnp.concatenate([*rest_parts[0], qkv_parts[1]], axis=1)
    rest_part = tie(rest_part, w_now)[0]
    state = tokens.astype(F32)
    saved = []
    for layer in range(LAYERS):
        shift = all_shifts[layer]
        zeros = jnp.zeros((OWN_HEADS, HEAD), F32)
        qkv_bias = jnp.stack(
            [
                pick(shift[2].reshape(OWN_HEADS, CORES, HEAD), 1),
                zeros,
                pick(shift[3].reshape(OWN_HEADS, CORES, HEAD), 1),
            ],
            axis=1,
        ).reshape(QKV_HALF)
        bias = pick(all_up[layer], 0).reshape(FF_HALF)
        few = (all_gains[layer], shift, qkv_bias, bias)
        state, kept, weights, rest = layer_forward(state, w_now, rest_part, few, core)
        if layer + 1 < LAYERS:
            w_now = rest[:, D + 2 * FF_HALF :]
            rest_part = jnp.concatenate(rest_parts[1], axis=1)
            rest_part = tie(rest_part, rest)[0]
        saved.append((kept, weights))
    output = state.astype(BF)
    grad = cotangent.astype(F32)
    grad, shares_one, rest_one, _ = layer_backward(*saved[1], grad, core, None)
    grad, shares, rest_two, early = layer_backward(*saved[0], grad, core, shares_one)
    rest = jnp.concatenate([ring_scatter(rest_one, "dp", 1), ring_scatter(rest_two, "dp", 1)], axis=1)
    late = chip_sum(jnp.concatenate([shares, rest], axis=1), LATE)
    pair = to_all_chips(jnp.concatenate([early, late], axis=1))
    grad_qkv, grad_out, grad_up, grad_down, small = unpack(core, *pair)
    return (
        output, grad, grad_qkv, grad_out, grad_up, grad_down,
        small[:, 0:2], small[:, 2:8], small[:, 8:12].reshape(LAYERS, FF // DP),
    )


def solution(mesh):
    placed = (
        P(("dp", "ctx"), None),
        P(("dp", "ctx"), None),
        P(None, "dp", None),
        P(None, "dp", None),
        P(None, "dp", None),
        P(None, "dp", None),
        P(None, None, "dp"),
        P(None, None, "dp"),
        P(None, "dp"),
    )
    return jax.shard_map(
        local,
        mesh=mesh,
        in_specs=placed,
        out_specs=placed,
        check_vma=False,
    )
```

```python
import jax
import jax.numpy as jnp
from jax import lax
from jax.experimental import pallas as pl
from jax.experimental.pallas import tpu as pltpu
from jax.sharding import PartitionSpec as P

HEADS = 12
HEAD = 64
LAYERS = 2
D = 768
FF = 3072
DP = 8
BLK = 128
CHIPS = 8
CORES = 2
PAIR = CORES * BLK
OWN_HEADS = HEADS // CORES
SEQ = CHIPS * PAIR
FF_PART = FF // DP // CORES
FF_HALF = FF // CORES
QKV_HALF = 3 * D // CORES
EPSILON = 1e-05
NEGATIVE = -1e30
EARLY = 4096
LATE = 6144
SAME_CORE = [[CORES * u + k for u in range(CHIPS)] for k in range(CORES)]
OTHER_CORE = [(i, i ^ 1) for i in range(CHIPS * CORES)]
BF = jnp.bfloat16
F32 = jnp.float32


def dot(left, right, ldim, rdim):
    return lax.dot_general(
        left, right, (((ldim,), (rdim,)), ((), ())), preferred_element_type=F32
    )


def ring(axis, step, scale):
    size = 4
    count = 2 * size * scale
    moves = []
    for i in range(count):
        block, low = i // scale, i % scale
        pair, at = block // size, block % size
        moves.append((i, (pair * size + (at + step) % size) * scale + low))
    return lambda value: lax.ppermute(value, axis, moves)


def across(axis, scale):
    count = 8 * scale
    return lambda value: lax.ppermute(
        value, axis, [(i, (i + count // 2) % count) for i in range(count)]
    )


def places(axis, scale):
    block = lax.axis_index(axis) // scale
    pair, at = block // 4, block % 4
    return [[((pair + far) % 2) * 4 + (at + step) % 4 for step in range(4)] for far in range(2)]


def gather_start(value, axis, scale):
    value = value[None]
    far = across(axis, scale)(value)
    own_up, own_down = ring(axis, 1, scale)(value), ring(axis, -1, scale)(value)
    return value, far, own_up, own_down


def gather_go_on(begun, axis, scale, after_one=None, after_two=None):
    if after_one is not None:
        begun = tie(begun, after_one)[0]
    value, far, own_up, own_down = begun
    up, down = ring(axis, 1, scale), ring(axis, -1, scale)
    far_up, far_down = up(far), down(far)
    own_two = up(own_up)
    if after_two is not None:
        far_down = tie(far_down, after_two)[0]
    far_two = down(far_down)
    return value, own_up, own_two, own_down, far, far_up, far_two, far_down


def join_kernel(where_ref, *refs):
    pieces, parts = refs[:8], refs[8:]
    for k in range(8):
        at = 0
        for part in parts:
            rows = part.shape[1]
            part[where_ref[k]] = pieces[k][0, at : at + rows]
            at += rows


def gather_end(pieces, axis, scale, *heights):
    where = places(axis, scale)
    where = jnp.stack([where[k // 4][-(k % 4) % 4] for k in range(8)]).astype(jnp.int32)
    _, rows, width = pieces[0].shape
    return pl.pallas_call(
        join_kernel,
        in_specs=[pl.BlockSpec(memory_space=pltpu.SMEM)]
        + [pl.BlockSpec(memory_space=pltpu.VMEM)] * 8,
        out_shape=[
            jax.ShapeDtypeStruct((8, height, width), pieces[0].dtype) for height in heights or (rows,)
        ],
        compiler_params=pltpu.CompilerParams(vmem_limit_bytes=40 * 1024 * 1024),
        name="join",
    )(where, *pieces)


def ring_scatter(value, axis, scale):
    up, down, pair = ring(axis, 1, scale), ring(axis, -1, scale), across(axis, scale)
    where = places(axis, scale)
    value = value.reshape(8, value.shape[0] // 8, *value.shape[1:])

    def part(far, step):
        return lax.dynamic_index_in_dim(value, where[far][step], 0, keepdims=False)

    def add(*terms):
        total = terms[0].astype(F32)
        for term in terms[1:]:
            total = total + term.astype(F32)
        return total.astype(BF)

    own_two, far_two = up(part(0, 2)), down(part(1, 2))
    far_up, own_down = up(part(1, 1)), down(part(0, 3))
    own_up = up(add(part(0, 1), own_two))
    far_down = down(add(part(1, 3), far_two))
    far = pair(add(part(1, 0), far_up, far_down))
    return add(part(0, 0), own_up, own_down, far)


def tie(*values):
    return lax.optimization_barrier(values)


def swap(value):
    return lax.ppermute(value, "ctx", OTHER_CORE)


def diagonal_mask(size):
    key = lax.broadcasted_iota(jnp.int32, (size, size), 0)
    query = lax.broadcasted_iota(jnp.int32, (size, size), 1)
    return key <= query


def attend_kernel(qkv_ref, out_ref, ctx_ref, lse_ref):
    step = PAIR
    keys = [qkv_ref[j, HEAD : 2 * HEAD, :] for j in range(CHIPS)]
    allowed = diagonal_mask(step)
    for i in range(CHIPS):
        query = qkv_ref[i, 0:HEAD, :]
        scores = [dot(keys[j], query, 0, 0) for j in range(i + 1)]
        scores[i] = jnp.where(allowed, scores[i], NEGATIVE)
        peak = scores[0].max(axis=0, keepdims=True)
        for j in range(1, i + 1):
            peak = jnp.maximum(peak, scores[j].max(axis=0, keepdims=True))
        total = jnp.zeros((1, step), F32)
        accum = jnp.zeros((HEAD, step), F32)
        for j in range(i + 1):
            weights = jnp.exp(scores[j] - peak)
            total = total + weights.sum(axis=0, keepdims=True)
            accum = accum + dot(qkv_ref[j, 2 * HEAD : 3 * HEAD, :], weights.astype(BF), 1, 0)
        context = accum / total
        out_ref[2 * i] = context[:, :BLK].astype(BF)
        out_ref[2 * i + 1] = context[:, BLK:].astype(BF)
        ctx_ref[i] = context
        lse_ref[i] = peak + jnp.log(total)


def attend(qkv):
    return pl.pallas_call(
        attend_kernel,
        out_shape=(
            jax.ShapeDtypeStruct((CORES * CHIPS, HEAD, BLK), BF),
            jax.ShapeDtypeStruct((CHIPS, HEAD, PAIR), F32),
            jax.ShapeDtypeStruct((CHIPS, 1, PAIR), F32),
        ),
        compiler_params=pltpu.CompilerParams(vmem_limit_bytes=40 * 1024 * 1024),
        name="attend",
    )(qkv)


def attend_back_kernel(qkv_ref, grad_ref, ctx_ref, lse_ref, out_ref, dq_ref):
    allowed = diagonal_mask(PAIR)
    grads, deltas = [], []
    for i in range(CHIPS):
        grad = jnp.concatenate([grad_ref[2 * i], grad_ref[2 * i + 1]], axis=1)
        grads.append(grad)
        deltas.append((grad.astype(F32) * ctx_ref[i]).sum(axis=0, keepdims=True))
    for j in range(CHIPS):
        key = qkv_ref[j, HEAD : 2 * HEAD, :]
        value = qkv_ref[j, 2 * HEAD : 3 * HEAD, :]
        grad_key = jnp.zeros((HEAD, PAIR), F32)
        grad_value = jnp.zeros((HEAD, PAIR), F32)
        for i in range(j, CHIPS):
            query = qkv_ref[i, 0:HEAD, :]
            probs = jnp.exp(dot(key, query, 0, 0) - lse_ref[i])
            if i == j:
                probs = jnp.where(allowed, probs, 0.0)
            grad_probs = dot(value, grads[i], 0, 0)
            grad_scores = (probs * (grad_probs - deltas[i])).astype(BF)
            grad_value = grad_value + dot(grads[i], probs.astype(BF), 1, 1)
            grad_key = grad_key + dot(query, grad_scores, 1, 1)
            grad_query = dot(key, grad_scores, 1, 0)
            if j == 0:
                dq_ref[i] = grad_query
            else:
                dq_ref[i] = dq_ref[i] + grad_query
        out_ref[j, 0:HEAD, :] = (dq_ref[j] * HEAD**-0.5).astype(BF)
        out_ref[j, HEAD : 2 * HEAD, :] = grad_key.astype(BF)
        out_ref[j, 2 * HEAD : 3 * HEAD, :] = grad_value.astype(BF)


def attend_back(qkv, grad, context, logsum):
    return pl.pallas_call(
        attend_back_kernel,
        out_shape=jax.ShapeDtypeStruct((CHIPS, 3 * HEAD, PAIR), BF),
        scratch_shapes=[pltpu.VMEM((CHIPS, HEAD, PAIR), F32)],
        compiler_params=pltpu.CompilerParams(vmem_limit_bytes=40 * 1024 * 1024),
        name="attend_back",
    )(qkv, grad, context, logsum)


def norm_parts(values):
    average = jnp.mean(values, axis=-1, keepdims=True)
    centered = values - average
    spread = jnp.mean(centered * centered, axis=-1, keepdims=True)
    scale = lax.rsqrt(spread + EPSILON)
    return centered * scale, scale


def norm_back(grad, hat, scale, gain):
    scaled = grad * gain
    first = jnp.mean(scaled, axis=-1, keepdims=True)
    second = jnp.mean(scaled * hat, axis=-1, keepdims=True)
    part = scale * (scaled - first - hat * second)
    return part, jnp.sum(grad * hat, axis=0), jnp.sum(grad, axis=0)


def ordered(mine, other, core):
    three = jnp.concatenate([mine, other, mine], axis=0)
    return lax.dynamic_slice_in_dim(three, core * BLK, PAIR, 0)


def across_chips(value):
    return lax.all_to_all(value, "ctx", 0, 0, axis_index_groups=SAME_CORE, tiled=True)


def layer_forward(state, w_qkv, rest_part, vectors, core):
    gains, shifts, qkv_bias, up_bias = vectors
    hat_one, scale_one = norm_parts(state)
    mine = (hat_one * gains[0] + shifts[0]).astype(BF)
    normed = ordered(mine, swap(mine), core)
    rest = gather_start(rest_part, "dp", 1)
    mixed = (dot(w_qkv, normed, 0, 1) + qkv_bias[:, None]).reshape(OWN_HEADS, 3, HEAD, PAIR)
    factor = jnp.array([HEAD**-0.5, 1.0, 1.0], F32).reshape(1, 3, 1, 1)
    qkv = (mixed * factor).astype(BF).reshape(OWN_HEADS, 3 * HEAD, PAIR)
    qkv = jnp.concatenate([qkv, jnp.zeros((CHIPS - OWN_HEADS, 3 * HEAD, PAIR), BF)], axis=0)
    qkv = across_chips(qkv)
    out, context, logsum = attend(qkv)
    rest = gather_go_on(rest, "dp", 1, qkv, out)
    out = lax.all_to_all(out, "ctx", 0, 0, tiled=True)
    rest = gather_end(rest, "dp", 1)[0].reshape(D, -1)
    w_out, w_up, w_down = rest[:, :D], rest[:, D : D + FF_HALF], rest[:, D + FF_HALF : D + 2 * FF_HALF]
    attended = out[:HEADS].reshape(D, BLK)
    middle = state + (dot(attended, w_out, 0, 0) + shifts[4])
    hat_two, scale_two = norm_parts(middle)
    mine_two = (hat_two * gains[1] + shifts[1]).astype(BF)
    normed_two = jnp.concatenate([mine_two, swap(mine_two)], axis=0)
    upper = dot(normed_two, w_up, 1, 0) + up_bias
    active = jax.nn.gelu(upper).astype(BF)
    partial = dot(active[:, :D], w_down[:, :D], 1, 0) + dot(active[:, D:], w_down[:, D:], 1, 0)
    result = middle + (partial[:BLK] + swap(partial[BLK:].astype(BF)).astype(F32) + shifts[5])
    kept = (
        hat_one, scale_one, normed, qkv, context, logsum,
        attended, hat_two, scale_two, normed_two, upper, active,
    )
    weights = (w_qkv, w_out, w_up, w_down, gains)
    return result, kept, weights, rest


def half_to_full(vector, parts, core):
    piece = vector.reshape(parts, 1, -1)
    slot = lax.broadcasted_iota(jnp.int32, (parts, CORES, piece.shape[2]), 1)
    return jnp.where(slot == core, piece, 0.0).reshape(-1)


def layer_backward(kept, weights, grad_result, core, earlier):
    (
        hat_one, scale_one, normed, qkv, context, logsum,
        attended, hat_two, scale_two, normed_two, upper, active,
    ) = kept
    w_qkv, w_out, w_up, w_down, gains = weights
    mine = grad_result.astype(BF)
    down_bias = jnp.sum(mine.astype(F32), axis=0)
    both = jnp.concatenate([mine, swap(mine)], axis=0)
    grad_active = jnp.concatenate(
        [dot(both, w_down[:, :D], 1, 1), dot(both, w_down[:, D:], 1, 1)], axis=1
    )
    gelu_back = jax.vjp(jax.nn.gelu, upper)[1]
    grad_upper = gelu_back(grad_active)[0].astype(BF)
    partial = dot(grad_upper, w_up, 1, 1)
    grad_normed_two = partial[:BLK] + swap(partial[BLK:].astype(BF)).astype(F32)
    grad_down = dot(active, both, 0, 0).astype(BF)
    grad_up = dot(normed_two, grad_upper, 0, 0).astype(BF)
    grad_upbias = jnp.sum(grad_upper.astype(F32), axis=0)
    part, gain_two, shift_two = norm_back(grad_normed_two, hat_two, scale_two, gains[1])
    grad_middle = grad_result + part
    branch = grad_middle.astype(BF)
    out_bias = jnp.sum(branch.astype(F32), axis=0)
    grad_out_t = dot(w_out, branch, 1, 1).astype(BF).reshape(HEADS, HEAD, BLK)
    grad_out_t = jnp.concatenate(
        [grad_out_t, jnp.zeros((CHIPS * CORES - HEADS, HEAD, BLK), BF)], axis=0
    )
    grad_context = lax.all_to_all(grad_out_t, "ctx", 0, 0, tiled=True)
    grad_out = dot(attended, branch, 1, 0)
    columns = D // CORES
    keep = lax.dynamic_slice_in_dim(grad_out, core * columns, columns, 1)
    give = lax.dynamic_slice_in_dim(grad_out, (1 - core) * columns, columns, 1)
    grad_out = (keep + swap(give.astype(BF)).astype(F32)).astype(BF)
    wide = jnp.concatenate([grad_up, grad_down[:D], grad_down[D:], grad_out], axis=1)
    grad_context, wide = tie(grad_context, wide)
    shares = lax.psum_scatter(wide, "dp", scatter_dimension=0, tiled=True)
    if earlier is not None:
        grad_context, earlier = tie(grad_context, earlier)
    grad_mixed = attend_back(qkv, grad_context, context, logsum)
    grad_mixed = across_chips(grad_mixed)
    grad_mixed = grad_mixed[:OWN_HEADS].reshape(QKV_HALF, PAIR)
    partial = dot(grad_mixed, w_qkv, 0, 1)
    mine = lax.dynamic_slice_in_dim(partial, core * BLK, BLK, 0)
    other = lax.dynamic_slice_in_dim(partial, (1 - core) * BLK, BLK, 0)
    grad_normed = mine + swap(other.astype(BF)).astype(F32)
    grad_qkv = dot(normed, grad_mixed, 0, 1).astype(BF)
    sums = jnp.sum(grad_mixed.astype(F32), axis=1).reshape(OWN_HEADS, 3, HEAD)
    part, gain_one, shift_one = norm_back(grad_normed, hat_one, scale_one, gains[0])
    grad_state = grad_middle + part
    upbias = grad_upbias.reshape(2, D)
    empty = jnp.zeros_like(upbias)
    upbias = jnp.concatenate(
        [jnp.where(core == 0, upbias, empty), jnp.where(core == 1, upbias, empty)], axis=0
    )
    small = jnp.stack(
        [
            gain_one, gain_two, shift_one, shift_two,
            half_to_full(sums[:, 0], OWN_HEADS, core), half_to_full(sums[:, 2], OWN_HEADS, core),
            out_bias, down_bias, upbias[0], upbias[1], upbias[2], upbias[3],
        ]
    )
    small = small + swap(small)
    small = jnp.pad(small.astype(BF).T, ((0, 0), (0, 128 - 12)))
    grad_rest = jnp.concatenate([grad_qkv, small], axis=1)
    if earlier is None:
        grad_state, grad_rest = tie(grad_state, grad_rest)
    return grad_state, shares, grad_rest, earlier


def chip_sum(shares, width):
    rows = D // DP
    shares = jnp.pad(shares, ((0, 0), (0, width - shares.shape[1])))
    pieces = shares.reshape(rows, CHIPS, width // CHIPS).transpose(1, 0, 2)
    moved = lax.all_to_all(pieces, "ctx", 0, 0, axis_index_groups=SAME_CORE, tiled=True)
    return jnp.sum(moved.astype(F32), axis=0).astype(BF)


def to_all_chips(summed):
    mine = gather_go_on(gather_start(summed, "ctx", CORES), "ctx", CORES)
    mine = gather_end(mine, "ctx", CORES)[0]
    return mine, swap(mine)


def unpack_kernel(core_ref, *refs):
    mine_ref, other_ref, qkv_ref, out_ref, up_ref, down_ref, small_ref, flat = refs
    rows = D // DP

    @pl.when(pl.program_id(0) == 0)
    def _():
        first = core_ref[0] == 0
        at = 0
        for start, size in ((0, EARLY // CHIPS), (EARLY // CHIPS, LATE // CHIPS)):
            for c in range(CHIPS):
                mine = mine_ref[c, :, start : start + size].astype(F32)
                other = other_ref[c, :, start : start + size].astype(F32)
                flat[0, :, at : at + size] = jnp.where(first, mine, other)
                flat[1, :, at : at + size] = jnp.where(first, other, mine)
                at += size

    def layer(mlp, rest):
        def part(k, start, size):
            low, high = start // 128 * 128, -(-(start + size) // 128) * 128
            return flat[k, :, low:high][:, start - low : start - low + size]

        for d in range(DP):
            pieces = [
                part(k, mlp + e * D + d * rows, rows) for k in range(CORES) for e in range(2)
            ]
            up_ref[0, :, d * 4 * rows : (d + 1) * 4 * rows] = jnp.concatenate(pieces, axis=1)
        for k in range(CORES):
            for e in range(2):
                at = mlp + FF_HALF + e * D
                down_ref[0, (2 * k + e) * rows : (2 * k + e + 1) * rows, :] = flat[k, :, at : at + D]
            at = mlp + 2 * FF_HALF
            out_ref[0, :, k * D // 2 : (k + 1) * D // 2] = flat[k, :, at : at + D // 2]
        for t in range(3):
            for u in range(OWN_HEADS):
                pieces = [part(k, rest + (u * 3 + t) * HEAD, HEAD) for k in range(CORES)]
                to = t * D + u * 2 * HEAD
                qkv_ref[0, :, to : to + 2 * HEAD] = jnp.concatenate(pieces, axis=1)
        small_ref[0] = flat[0, :, rest + QKV_HALF : rest + QKV_HALF + 128].T[:16]

    late = EARLY + 2 * FF_HALF + D // 2
    pl.when(pl.program_id(0) == 0)(lambda: layer(EARLY, late + QKV_HALF + 128))
    pl.when(pl.program_id(0) == 1)(lambda: layer(0, late))


def unpack(core, *pairs):
    rows = D // DP
    shapes = [(rows, 3 * D), (rows, D), (rows, FF), (FF // DP, D), (16, rows)]
    return pl.pallas_call(
        unpack_kernel,
        grid=(LAYERS,),
        in_specs=[pl.BlockSpec(memory_space=pltpu.SMEM)]
        + [pl.BlockSpec(pair.shape, lambda i: (0, 0, 0)) for pair in pairs],
        out_specs=[pl.BlockSpec((1, *shape), lambda i: (i, 0, 0)) for shape in shapes],
        out_shape=[jax.ShapeDtypeStruct((LAYERS, *shape), F32) for shape in shapes],
        scratch_shapes=[pltpu.VMEM((CORES, rows, EARLY + LATE), F32)],
        compiler_params=pltpu.CompilerParams(vmem_limit_bytes=48 * 1024 * 1024),
        name="unpack",
    )(core.reshape(1), *pairs)


def local(tokens, cotangent, w_qkv, w_out, w_up, w_down, gains, shifts, up_bias):
    core = lax.rem(lax.axis_index("ctx"), CORES)
    rows = D // DP

    def pick(value, axis):
        return lax.dynamic_index_in_dim(value, core, axis, keepdims=False)

    vectors = jnp.concatenate(
        [gains.reshape(-1, rows), shifts.reshape(-1, rows), up_bias.reshape(-1, rows)], axis=0
    )
    vectors = jnp.pad(vectors.reshape(2, QKV_HALF), ((0, 14), (0, 0)))
    weights = []
    qkv_parts, rest_parts = [], []
    for layer in range(LAYERS):
        qkv_part = pick(w_qkv[layer].reshape(rows, 3, OWN_HEADS, CORES, HEAD), 3)
        qkv_parts.append(qkv_part.transpose(0, 2, 1, 3).reshape(rows, QKV_HALF))
        up = pick(w_up[layer].reshape(rows, DP, CORES, 2, rows), 2)
        up = up.transpose(0, 2, 1, 3).reshape(rows, FF_HALF)
        down = pick(w_down[layer].reshape(CORES, 2, rows, D), 0)
        rest_parts.append([w_out[layer], up, down[0], down[1]])
    first = gather_start(jnp.concatenate([qkv_parts[0], vectors], axis=0), "dp", 1)
    first, vectors = gather_end(gather_go_on(first, "dp", 1), "dp", 1, rows, 16)
    vectors = vectors[:, :2].reshape(DP, 24, rows).transpose(1, 0, 2).astype(F32)
    all_gains = vectors[:4].reshape(LAYERS, 2, D)
    all_shifts = vectors[4:16].reshape(LAYERS, 6, D)
    all_up = vectors[16:24].reshape(LAYERS, CORES, 2, DP, rows)
    w_now = first.reshape(D, QKV_HALF)
    rest_part = jnp.concatenate([*rest_parts[0], qkv_parts[1]], axis=1)
    rest_part = tie(rest_part, w_now)[0]
    state = tokens.astype(F32)
    saved = []
    for layer in range(LAYERS):
        shift = all_shifts[layer]
        zeros = jnp.zeros((OWN_HEADS, HEAD), F32)
        qkv_bias = jnp.stack(
            [
                pick(shift[2].reshape(OWN_HEADS, CORES, HEAD), 1),
                zeros,
                pick(shift[3].reshape(OWN_HEADS, CORES, HEAD), 1),
            ],
            axis=1,
        ).reshape(QKV_HALF)
        bias = pick(all_up[layer], 0).reshape(FF_HALF)
        few = (all_gains[layer], shift, qkv_bias, bias)
        state, kept, weights, rest = layer_forward(state, w_now, rest_part, few, core)
        if layer + 1 < LAYERS:
            w_now = rest[:, D + 2 * FF_HALF :]
            rest_part = jnp.concatenate(rest_parts[1], axis=1)
            rest_part = tie(rest_part, rest)[0]
        saved.append((kept, weights))
    output = state.astype(BF)
    grad = cotangent.astype(F32)
    grad, shares_one, rest_one, _ = layer_backward(*saved[1], grad, core, None)
    grad, shares, rest_two, early = layer_backward(*saved[0], grad, core, shares_one)
    early = chip_sum(tie(early, rest_two)[0], EARLY)
    rest = jnp.concatenate([ring_scatter(rest_one, "dp", 1), ring_scatter(rest_two, "dp", 1)], axis=1)
    late = chip_sum(jnp.concatenate([shares, rest], axis=1), LATE)
    pair = to_all_chips(jnp.concatenate([early, late], axis=1))
    grad_qkv, grad_out, grad_up, grad_down, small = unpack(core, *pair)
    return (
        output, grad, grad_qkv, grad_out, grad_up, grad_down,
        small[:, 0:2], small[:, 2:8], small[:, 8:12].reshape(LAYERS, FF // DP),
    )


def solution(mesh):
    placed = (
        P(("dp", "ctx"), None),
        P(("dp", "ctx"), None),
        P(None, "dp", None),
        P(None, "dp", None),
        P(None, "dp", None),
        P(None, "dp", None),
        P(None, None, "dp"),
        P(None, None, "dp"),
        P(None, "dp"),
    )
    return jax.shard_map(
        local,
        mesh=mesh,
        in_specs=placed,
        out_specs=placed,
        check_vma=False,
    )
```
